256 devices in a mesh: dom: 32 (over y, z), dir: 8 (over x, core).
Axes of the slice: x: 4, y: 4, z: 8, core: 2. Of those that a mesh axis runs over, the one named last changes fastest.
Arguments:
- incident: bfloat16 [2048, 128, 512], P('dom', 'dir'), may hold values from -6 to 6
- cotangent: bfloat16 [2048, 128, 512], P('dom', 'dir'), may hold values from -6 to 6
- mie: float32 [2048, 512], P('dom'), may hold values from 0.2 to 1
- trans: bfloat16 [12, 512, 512], replicated, may hold values from -0.25 to 0.25
- send_rows: int32 [32, 32, 8], P('dom'), may hold values from 0 to 63, as said below
- partner_slot: int32 [2048, 12], P('dom'), may hold values from -1 to 319, as said below
Outputs:
- amplitude: bfloat16 [2048, 128, 512], P('dom', 'dir')
- gradient: float32 [2048, 512], P('dom', 'dir')
The draws below stay inside these ranges and needn't reach their ends.
Inputs may be any that keep to these rules, and one draw needn't show every extreme that they name: Within each block send_rows[q, d, :] the rows are distinct; over all d every row of device q appears. `partner_slot`: among the rows of one device, every value from 64 to 319 appears exactly once; values below 64 never name the row's own particle; each device has one or more -1 entries.
All inputs are finite; a program needn't handle non-finite values.
Results may differ from the reference program's by a relative error of at most 0.0045.
Values may be sent and summed in bfloat16 or wider, within the bound.
No kernel may reach another device: no remote copies, remote signals or barrier semaphores. Data moves between devices by JAX's collectives and lax.ppermute only.
A program may use at most 128 MiB of HBM per device.

```python
import jax
import jax.numpy as jnp
from jax import lax

C = 512
K = 12
P_DEV = 64
CAP = 8
PARTICLES = 2048
DIRS = 128
N_DOM = 32


def draw_send_rows(key, part):
    key = jax.random.fold_in(key, 3)
    source_keys = jax.random.split(key, N_DOM)
    orders = jax.vmap(lambda one_key: jax.random.permutation(one_key, P_DEV))(source_keys)
    position = (jnp.arange(N_DOM)[:, None] * CAP + jnp.arange(CAP)[None, :]) % P_DEV
    return orders[:, position].astype(jnp.int32)


def draw_partner_slot(key, part):
    key = jax.random.fold_in(key, 7)
    key_rank, key_gap, key_off = jax.random.split(key, 3)
    ref_count = P_DEV * K
    remote_count = N_DOM * CAP
    ranks = jax.vmap(lambda one_key: jax.random.permutation(one_key, ref_count))(jax.random.split(key_rank, N_DOM))
    vacant = jax.random.randint(key_gap, (N_DOM, 1), 1, (ref_count - remote_count) // 2 + 1)
    offsets = jax.random.randint(key_off, (N_DOM, ref_count), 1, P_DEV)
    own_row = jnp.arange(ref_count) // K
    local_row = (own_row[None, :] + offsets) % P_DEV
    values = jnp.where(ranks < remote_count, P_DEV + ranks, jnp.where(ranks < remote_count + vacant, -1, local_row))
    return values.reshape(N_DOM * P_DEV, K).astype(jnp.int32)


def shard_levels(own_key, dims, cuts, low, largest):
    level, own = 1.0, jax.random.fold_in(own_key, 6)
    for dim, blocks in cuts:
        steps = jnp.exp(jax.random.uniform(jax.random.fold_in(own, dim), (blocks,), jnp.float32, low / len(cuts), largest / len(cuts)))
        level = level * jnp.repeat(steps, dims[dim] // blocks).reshape([-1 if axis == dim else 1 for axis in range(len(dims))])
    return level


def scatter_about(key, dims, scale, reach, pieces=(), held_as=jnp.bfloat16):
    array = jax.random.normal(key, dims, jnp.float32) * scale
    if len(pieces) > 0:
        array = shard_levels(key, dims, pieces, -0.22, 0.18) * array
    return jnp.clip(array, min=-reach, max=reach).astype(held_as)


def setup_inputs(seed: int = 0) -> dict:
    streams_of = jax.random.split(jax.random.key(seed), 7)
    incident = scatter_about(streams_of[0], (PARTICLES, DIRS, C), 1.0, 6.0, ((0, 32), (1, 8)))
    cotangent = scatter_about(streams_of[1], (PARTICLES, DIRS, C), 1.0, 6.0, ((0, 32), (1, 8)))
    mie = jnp.clip(0.2 + 0.8 * jax.random.uniform(streams_of[2], (PARTICLES, C), jnp.float32) ** shard_levels(streams_of[2], (PARTICLES, C), ((0, 32),), -0.2, 0.2), 0.2, 1.0)
    trans = scatter_about(streams_of[3], (K, C, C), C ** -0.5, 0.25)
    send_rows = draw_send_rows(jax.random.fold_in(streams_of[6], 71), 0)
    partner_slot = draw_partner_slot(jax.random.fold_in(streams_of[6], 71), 0)
    return {"incident": incident, "cotangent": cotangent, "mie": mie, "trans": trans, "send_rows": send_rows, "partner_slot": partner_slot}


def reference(incident, cotangent, mie, trans, send_rows, partner_slot):
    n_part = incident.shape[0]
    owner_dev = (jnp.arange(n_part, dtype=jnp.int32) // P_DEV)[:, None]
    slot_val = partner_slot
    remote_slot = jnp.clip(slot_val - P_DEV, 0, N_DOM * CAP - 1)
    source_dev = remote_slot // CAP
    source_pos = remote_slot % CAP
    remote_id = source_dev * P_DEV + send_rows[source_dev, owner_dev, source_pos]
    local_id = owner_dev * P_DEV + jnp.clip(slot_val, 0, P_DEV - 1)
    partner = jnp.where(slot_val < 0, n_part, jnp.where(slot_val < P_DEV, local_id, remote_id)).astype(jnp.int32)
    mie_col = mie[:, None, :]
    start_amp = (mie_col * incident.astype(jnp.float32)).astype(jnp.bfloat16)
    adj_amp = (mie_col * cotangent.astype(jnp.float32)).astype(jnp.bfloat16)
    padded = jnp.concatenate([start_amp, jnp.zeros((1,) + start_amp.shape[1:], jnp.bfloat16)], axis=0)

    def forward_class(carry_sum, class_item):
        matrix, slot_col = class_item
        picked = padded[slot_col].astype(jnp.float32)
        return carry_sum + jnp.einsum("pnc,cd->pnd", picked, matrix.astype(jnp.float32)), None

    total_field, _ = lax.scan(forward_class, incident.astype(jnp.float32), (trans, partner.T))
    amplitude = (mie_col * total_field).astype(jnp.bfloat16)
    adj_float = adj_amp.astype(jnp.float32)

    def backward_class(carry_sum, class_item):
        matrix, slot_col = class_item
        products = jnp.einsum("pnc,dc->pnd", adj_float, matrix.astype(jnp.float32))
        return carry_sum.at[slot_col].add(products), None

    empty_sum = jnp.zeros((n_part + 1,) + incident.shape[1:], jnp.float32)
    adjoint_full, _ = lax.scan(backward_class, empty_sum, (trans, partner.T))
    adjoint = adjoint_full[:n_part]
    summed = jnp.sum(cotangent.astype(jnp.float32) * total_field + incident.astype(jnp.float32) * adjoint, axis=1)
    gradient = summed / DIRS
    return amplitude, gradient
```

```python
import functools

import jax
import jax.numpy as jnp
from jax import lax
from jax.experimental import pallas as pl
from jax.experimental.pallas import tpu as pltpu
from jax.sharding import PartitionSpec as P

CHUNKS = 2
TILE = 8
F32 = jnp.float32
BF16 = jnp.bfloat16
MIB = 1 << 20


def vmem():
    return pl.BlockSpec(memory_space=pltpu.VMEM)


def smem():
    return pl.BlockSpec(memory_space=pltpu.SMEM)


def pack_rows(rows_ref, mie_ref, inc_ref, out_ref):
    def one(i, carry):
        row = rows_ref[i]
        scaled = mie_ref[pl.ds(row, 1), :] * inc_ref[row].astype(F32)
        out_ref[i] = scaled.astype(BF16)
        return carry

    lax.fori_loop(0, out_ref.shape[0], one, 0, unroll=8)


def local_part(
    classes,
    chunk_rows,
    slot_ref,
    inc_ref,
    cot_ref,
    mie_ref,
    trans_ref,
    field_ref,
    back_refs,
    grad_ref,
    order_ref,
    count_ref,
    start_ref,
    adj_ref,
    lhs_ref,
    prod_ref,
    table_ref,
):
    count_p, count_n, width = inc_ref.shape
    chunks = len(back_refs)
    stride = count_p + TILE
    dummy = table_ref.shape[0] - 1

    def prepare(p, carry):
        scale = mie_ref[pl.ds(p, 1), :]
        inc = inc_ref[p].astype(F32)
        start_ref[p] = (scale * inc).astype(BF16)
        at = pl.multiple_of(p * count_n, count_n)
        adj_ref[pl.ds(at, count_n), :] = (scale * cot_ref[p].astype(F32)).astype(BF16)
        field_ref[pl.ds(at, count_n), :] = inc
        return carry

    lax.fori_loop(0, count_p, prepare, 0, unroll=4)
    start_ref[count_p] = jnp.zeros((count_n, width), BF16)

    def clear(t, carry):
        table_ref[t] = jnp.zeros((count_n, width), F32)
        return carry

    lax.fori_loop(0, dummy + 1, clear, 0, unroll=4)

    def one_class(k, carry):
        def pick(p, tallies):
            slot = slot_ref[p * classes + k]
            is_local = (slot >= 0) & (slot < count_p)
            source = jnp.where(is_local, slot, count_p)
            at = pl.multiple_of(p * count_n, count_n)
            lhs_ref[pl.ds(at, count_n), :] = start_ref[source]
            remote = slot - count_p
            fresh = []
            for h in range(chunks):
                tally = tallies[h]
                here = (remote >= h * chunk_rows) & (remote < (h + 1) * chunk_rows)
                order_ref[(h * classes + k) * stride + tally] = (
                    remote - h * chunk_rows
                ) * 128 + p
                fresh.append(tally + here.astype(jnp.int32))
            return tuple(fresh)

        tallies = lax.fori_loop(
            0, count_p, pick, tuple(jnp.int32(0) for _ in range(chunks)), unroll=4
        )
        for h in range(chunks):
            count_ref[h * classes + k] = tallies[h]
            for extra in range(TILE):
                order_ref[(h * classes + k) * stride + tallies[h] + extra] = count_p
        field_ref[...] += jnp.dot(lhs_ref[...], trans_ref[k], preferred_element_type=F32)
        prod_ref[...] = lax.dot_general(
            adj_ref[...],
            trans_ref[k],
            (((1,), (1,)), ((), ())),
            preferred_element_type=F32,
        )

        def spread(p, c):
            slot = slot_ref[p * classes + k]
            target = jnp.where(slot >= 0, slot, dummy)
            at = pl.multiple_of(p * count_n, count_n)
            table_ref[target] += prod_ref[pl.ds(at, count_n), :]
            return c

        lax.fori_loop(0, count_p, spread, 0, unroll=4)
        return carry

    lax.fori_loop(0, classes, one_class, 0)

    def finish(p, carry):
        grad_ref[pl.ds(p, 1), :] = jnp.sum(
            inc_ref[p].astype(F32) * table_ref[p], axis=0, keepdims=True
        )
        return carry

    lax.fori_loop(0, count_p, finish, 0, unroll=4)
    for h in range(chunks):

        def export(i, carry, h=h):
            back_refs[h][i] = table_ref[count_p + h * chunk_rows + i].astype(BF16)
            return carry

        lax.fori_loop(0, chunk_rows, export, 0, unroll=4)


def remote_part(
    classes,
    last,
    order_ref,
    count_ref,
    arrived_ref,
    back_ref,
    field_ref,
    trans_ref,
    *rest,
):
    if last:
        cot_ref, mie_ref, part_ref, amp_ref, grad_ref, term_ref, acc_ref, lhs_ref = rest
    else:
        out_ref, term_ref, acc_ref, lhs_ref = rest
    rows_in, count_n, width = arrived_ref.shape
    total = field_ref.shape[0]
    count_p = total // count_n
    stride = count_p + TILE

    def term(i, carry):
        at = pl.multiple_of(i * 8, 8)
        both = arrived_ref[pl.ds(at, 8)].astype(F32) * back_ref[pl.ds(at, 8)].astype(F32)
        term_ref[pl.ds(at, 8), :] = jnp.sum(both, axis=1)
        return carry

    lax.fori_loop(0, rows_in // 8, term, 0)
    acc_ref[pl.ds(0, total), :] = field_ref[...]

    def one_class(k, carry):
        def one_tile(t, c):
            base = k * stride + t * TILE
            for i in range(TILE):
                source = lax.shift_right_logical(order_ref[base + i], 7)
                lhs_ref[pl.ds(i * count_n, count_n), :] = arrived_ref[source]
            moved = jnp.dot(lhs_ref[...], trans_ref[k], preferred_element_type=F32)
            for i in range(TILE):
                p = order_ref[base + i] & 127
                at = pl.multiple_of(p * count_n, count_n)
                acc_ref[pl.ds(at, count_n), :] += moved[i * count_n : (i + 1) * count_n]
            return c

        tiles = lax.shift_right_logical(count_ref[k] + (TILE - 1), 3)
        lax.fori_loop(0, tiles, one_tile, 0)
        return carry

    lax.fori_loop(0, classes, one_class, 0)
    if not last:
        out_ref[...] = acc_ref[pl.ds(0, total), :]
        return

    def finish(p, carry):
        at = pl.multiple_of(p * count_n, count_n)
        field = acc_ref[pl.ds(at, count_n), :]
        amp_ref[p] = (mie_ref[pl.ds(p, 1), :] * field).astype(BF16)
        grad_ref[pl.ds(p, 1), :] = part_ref[pl.ds(p, 1), :] + jnp.sum(
            cot_ref[p].astype(F32) * field, axis=0, keepdims=True
        )
        return carry

    lax.fori_loop(0, count_p, finish, 0, unroll=4)


def combine(scale, rows_ref, mie_ref, part_ref, *rest):
    term_refs, out_ref, acc_ref = rest[:-2], rest[-2], rest[-1]
    acc_ref[...] = jnp.zeros_like(acc_ref)
    per = term_refs[0].shape[0]
    for h, term_ref in enumerate(term_refs):

        def one(i, carry, h=h, term_ref=term_ref):
            row = rows_ref[h * per + i]
            acc_ref[pl.ds(row, 1), :] += term_ref[pl.ds(i, 1), :]
            return carry

        lax.fori_loop(0, per, one, 0, unroll=8)
    out_ref[...] = (part_ref[...] + acc_ref[...] / mie_ref[...]) * scale


def body(incident, cotangent, mie, trans, send_rows, partner_slot):
    count_p, count_n, width = incident.shape
    classes = trans.shape[0]
    peers = lax.axis_size("dom")
    dirs = lax.axis_size("dir")
    cap = send_rows.shape[2]
    share = cap // CHUNKS
    chunk_rows = peers * share
    remote_rows = peers * cap
    total = count_p * count_n

    rows = send_rows[0].reshape(peers, CHUNKS, share).transpose(1, 0, 2).reshape(CHUNKS, chunk_rows)
    remote = partner_slot - count_p
    moved = (
        count_p
        + ((remote % cap) // share) * chunk_rows
        + (remote // cap) * share
        + remote % share
    )
    slots = jnp.where(remote >= 0, moved, partner_slot).reshape(-1)

    block = jax.ShapeDtypeStruct((chunk_rows, count_n, width), BF16)
    arrived = []
    for h in range(CHUNKS):
        packed = pl.pallas_call(
            pack_rows,
            out_shape=block,
            in_specs=[smem(), vmem(), vmem()],
            out_specs=vmem(),
            compiler_params=pltpu.CompilerParams(vmem_limit_bytes=8 * MIB),
            cost_estimate=pl.CostEstimate(
                flops=chunk_rows * count_n * width, bytes_accessed=6 * MIB, transcendentals=0
            ),
            name="pack_rows",
        )(rows[h], mie, incident)
        got = lax.all_to_all(
            packed.reshape(peers, share, count_n, width), "dom", split_axis=0, concat_axis=0, tiled=True
        )
        arrived.append(got.reshape(chunk_rows, count_n, width))

    stride = count_p + TILE
    field, back, part, order, count = pl.pallas_call(
        functools.partial(local_part, classes, chunk_rows),
        out_shape=(
            jax.ShapeDtypeStruct((total, width), F32),
            [block] * CHUNKS,
            jax.ShapeDtypeStruct((count_p, width), F32),
            jax.ShapeDtypeStruct((CHUNKS * classes * stride,), jnp.int32),
            jax.ShapeDtypeStruct((CHUNKS * classes,), jnp.int32),
        ),
        in_specs=[smem(), vmem(), vmem(), vmem(), vmem()],
        out_specs=(vmem(), [vmem()] * CHUNKS, vmem(), smem(), smem()),
        scratch_shapes=[
            pltpu.VMEM((count_p + 1, count_n, width), BF16),
            pltpu.VMEM((total, width), BF16),
            pltpu.VMEM((total, width), BF16),
            pltpu.VMEM((total, width), F32),
            pltpu.VMEM((count_p + remote_rows + 1, count_n, width), F32),
        ],
        compiler_params=pltpu.CompilerParams(vmem_limit_bytes=44 * MIB),
        cost_estimate=pl.CostEstimate(
            flops=4 * classes * total * width * width, bytes_accessed=20 * MIB, transcendentals=0
        ),
        name="local_part",
    )(slots, incident, cotangent, mie, trans)
    order = order.reshape(CHUNKS, classes * stride)
    count = count.reshape(CHUNKS, classes)

    returned = []
    for h in range(CHUNKS):
        last = h == CHUNKS - 1
        term_shape = jax.ShapeDtypeStruct((chunk_rows, width), F32)
        if last:
            out_shape = (
                jax.ShapeDtypeStruct((count_p, count_n, width), BF16),
                jax.ShapeDtypeStruct((count_p, width), F32),
                term_shape,
            )
            extra = (cotangent, mie, part)
        else:
            out_shape = (jax.ShapeDtypeStruct((total, width), F32), term_shape)
            extra = ()
        results = pl.pallas_call(
            functools.partial(remote_part, classes, last),
            out_shape=out_shape,
            in_specs=[smem(), smem()] + [vmem()] * (4 + len(extra)),
            out_specs=(vmem(),) * len(out_shape),
            scratch_shapes=[
                pltpu.VMEM((total + count_n, width), F32),
                pltpu.VMEM((TILE * count_n, width), BF16),
            ],
            compiler_params=pltpu.CompilerParams(vmem_limit_bytes=28 * MIB),
            cost_estimate=pl.CostEstimate(
                flops=2 * chunk_rows * count_n * width * width, bytes_accessed=14 * MIB, transcendentals=0
            ),
            name="remote_part",
        )(order[h], count[h], arrived[h], back[h], field, trans, *extra)
        if last:
            amplitude, part, term = results
        else:
            field, term = results
        term = lax.all_to_all(
            term.reshape(peers, share, width), "dom", split_axis=0, concat_axis=0, tiled=True
        )
        returned.append(term.reshape(chunk_rows, width))

    mine = pl.pallas_call(
        functools.partial(combine, 1.0 / (count_n * dirs)),
        out_shape=jax.ShapeDtypeStruct((count_p, width), F32),
        in_specs=[smem()] + [vmem()] * (2 + CHUNKS),
        out_specs=vmem(),
        scratch_shapes=[pltpu.VMEM((count_p, width), F32)],
        compiler_params=pltpu.CompilerParams(vmem_limit_bytes=8 * MIB),
        name="combine",
    )(rows.reshape(-1), mie, part, *returned)
    shares = mine.reshape(count_p, dirs, width // dirs).transpose(1, 0, 2)
    shares = lax.all_to_all(shares, "dir", split_axis=0, concat_axis=0, tiled=True)
    return amplitude, jnp.sum(shares, axis=0)


def solution(mesh):
    placed = (
        P("dom", "dir", None),
        P("dom", "dir", None),
        P("dom", None),
        P(),
        P("dom", None, None),
        P("dom", None),
    )
    return jax.shard_map(
        body,
        mesh=mesh,
        in_specs=placed,
        out_specs=(P("dom", "dir", None), P("dom", "dir")),
        check_vma=False,
    )
```

```python
import functools

import jax
import jax.numpy as jnp
from jax import lax
from jax.experimental import pallas as pl
from jax.experimental.pallas import tpu as pltpu
from jax.sharding import PartitionSpec as P

SPLITS = (0, 6, 8)
TILE = 8
F32 = jnp.float32
BF16 = jnp.bfloat16
MIB = 1 << 20


def vmem():
    return pl.BlockSpec(memory_space=pltpu.VMEM)


def smem():
    return pl.BlockSpec(memory_space=pltpu.SMEM)


def hbm():
    return pl.BlockSpec(memory_space=pl.ANY)


def pack_rows(low, rows_ref, mie_hbm, inc_hbm, out_hbm, mie_ref, inc_ref, out_ref, in_sem, out_sem):
    parts, part_peers, width = out_sem.shape[0], out_ref.shape[0] // out_sem.shape[0], out_ref.shape[1]
    get_mie = pltpu.make_async_copy(mie_hbm, mie_ref, in_sem.at[0])
    get_inc = pltpu.make_async_copy(inc_hbm, inc_ref, in_sem.at[1])
    get_mie.start()
    get_inc.start()
    get_mie.wait()
    get_inc.wait()

    def put(part):
        here = pl.ds(part * part_peers, part_peers)
        return pltpu.make_async_copy(out_ref.at[here], out_hbm.at[here], out_sem.at[part])

    for part in range(parts):

        def one(i, carry, part=part):
            peer = part * part_peers + i
            for c in range(width):
                row = rows_ref[low + c, peer]
                scaled = mie_ref[pl.ds(row, 1), :] * inc_ref[row].astype(F32)
                out_ref[peer, c] = scaled.astype(BF16)
            return carry

        lax.fori_loop(0, part_peers, one, 0, unroll=2)
        put(part).start()
    for part in range(parts):
        put(part).wait()


def local_part(
    cap,
    slot_ref,
    inc_ref,
    cot_ref,
    mie_ref,
    trans_ref,
    field_ref,
    back_ref,
    grad_ref,
    order_ref,
    count_ref,
    start_ref,
    adj_ref,
    lhs_ref,
    prod_ref,
    adjoint_ref,
):
    count_p, count_n, width = inc_ref.shape
    classes = slot_ref.shape[0]
    chunks = len(SPLITS) - 1
    stride = count_p + TILE
    dummy = back_ref.shape[0] - 1

    def prepare(p, carry):
        scale = mie_ref[pl.ds(p, 1), :]
        inc = inc_ref[p].astype(F32)
        start_ref[p] = (scale * inc).astype(BF16)
        at = pl.multiple_of(p * count_n, count_n)
        adj_ref[pl.ds(at, count_n), :] = (scale * cot_ref[p].astype(F32)).astype(BF16)
        field_ref[pl.ds(at, count_n), :] = inc
        adjoint_ref[p] = jnp.zeros((count_n, width), F32)
        return carry

    lax.fori_loop(0, count_p, prepare, 0, unroll=4)
    start_ref[count_p] = jnp.zeros((count_n, width), BF16)
    adjoint_ref[count_p] = jnp.zeros((count_n, width), F32)

    def one_class(k, carry):
        def pick(p, tallies):
            slot = slot_ref[k, p]
            is_local = (slot >= 0) & (slot < count_p)
            source = jnp.where(is_local, slot, count_p)
            at = pl.multiple_of(p * count_n, count_n)
            lhs_ref[pl.ds(at, count_n), :] = start_ref[source]
            remote = slot - count_p
            peer = lax.div(remote, cap)
            place = remote - peer * cap
            fresh = []
            for h in range(chunks):
                low, high = SPLITS[h], SPLITS[h + 1]
                here = (remote >= 0) & (place >= low) & (place < high)
                index = peer * (high - low) + place - low
                order_ref[(h * classes + k) * stride + tallies[h]] = index * 128 + p
                fresh.append(tallies[h] + here.astype(jnp.int32))
            return tuple(fresh)

        tallies = lax.fori_loop(
            0, count_p, pick, tuple(jnp.int32(0) for _ in range(chunks)), unroll=4
        )
        for h in range(chunks):
            count_ref[h * classes + k] = tallies[h]
            for extra in range(TILE):
                order_ref[(h * classes + k) * stride + tallies[h] + extra] = count_p
        field_ref[...] += jnp.dot(lhs_ref[...], trans_ref[k], preferred_element_type=F32)
        prod_ref[...] = lax.dot_general(
            adj_ref[...],
            trans_ref[k],
            (((1,), (1,)), ((), ())),
            preferred_element_type=F32,
        )

        def spread(p, c):
            slot = slot_ref[k, p]
            is_local = (slot >= 0) & (slot < count_p)
            at = pl.multiple_of(p * count_n, count_n)
            prod = prod_ref[pl.ds(at, count_n), :]
            back_ref[jnp.where(slot >= count_p, slot - count_p, dummy)] = prod.astype(BF16)
            adjoint_ref[jnp.where(is_local, slot, count_p)] += prod
            return c

        lax.fori_loop(0, count_p, spread, 0, unroll=4)
        return carry

    lax.fori_loop(0, classes, one_class, 0)

    def finish(p, carry):
        grad_ref[pl.ds(p, 1), :] = jnp.sum(
            inc_ref[p].astype(F32) * adjoint_ref[p], axis=0, keepdims=True
        )
        return carry

    lax.fori_loop(0, count_p, finish, 0, unroll=4)


def remote_part(
    classes,
    h,
    cap,
    order_ref,
    count_ref,
    arrived_ref,
    back_ref,
    field_ref,
    trans_ref,
    *rest,
):
    last = h == len(SPLITS) - 2
    if last:
        cot_ref, mie_ref, part_ref, before_ref, amp_ref, grad_ref, term_ref, acc_ref, lhs_ref = rest
        term_ref[...] = before_ref[...]
    else:
        out_ref, term_ref, acc_ref, lhs_ref = rest
    low, high = SPLITS[h], SPLITS[h + 1]
    rows_in, count_n, width = arrived_ref.shape
    peers, share = rows_in // (high - low), high - low
    total = field_ref.shape[0]
    count_p = total // count_n
    stride = count_p + TILE
    first = h * classes

    def term(q, carry):
        got = arrived_ref[pl.ds(q * share, share)].astype(F32)
        kept = back_ref[pl.ds(q * cap + low, share)].astype(F32)
        term_ref[q, low:high] = jnp.sum(got * kept, axis=1)
        return carry

    lax.fori_loop(0, peers, term, 0)
    acc_ref[pl.ds(0, total), :] = field_ref[...]

    def one_class(k, carry):
        def one_tile(t, c):
            base = (first + k) * stride + t * TILE
            for i in range(TILE):
                source = lax.shift_right_logical(order_ref[base + i], 7)
                lhs_ref[pl.ds(i * count_n, count_n), :] = arrived_ref[source]
            moved = jnp.dot(lhs_ref[...], trans_ref[k], preferred_element_type=F32)
            for i in range(TILE):
                p = order_ref[base + i] & 127
                at = pl.multiple_of(p * count_n, count_n)
                acc_ref[pl.ds(at, count_n), :] += moved[i * count_n : (i + 1) * count_n]
            return c

        tiles = lax.shift_right_logical(count_ref[first + k] + (TILE - 1), 3)
        lax.fori_loop(0, tiles, one_tile, 0)
        return carry

    lax.fori_loop(0, classes, one_class, 0)
    if not last:
        out_ref[...] = acc_ref[pl.ds(0, total), :]
        return

    def finish(p, carry):
        at = pl.multiple_of(p * count_n, count_n)
        field = acc_ref[pl.ds(at, count_n), :]
        amp_ref[p] = (mie_ref[pl.ds(p, 1), :] * field).astype(BF16)
        grad_ref[pl.ds(p, 1), :] = part_ref[pl.ds(p, 1), :] + jnp.sum(
            cot_ref[p].astype(F32) * field, axis=0, keepdims=True
        )
        return carry

    lax.fori_loop(0, count_p, finish, 0, unroll=4)


def combine(scale, rows_ref, mie_ref, part_ref, term_ref, out_ref, acc_ref):
    acc_ref[...] = jnp.zeros_like(acc_ref)

    def one(q, carry):
        for c in range(term_ref.shape[1]):
            row = rows_ref[c, q]
            acc_ref[pl.ds(row, 1), :] += term_ref[q, pl.ds(c, 1), :]
        return carry

    lax.fori_loop(0, term_ref.shape[0], one, 0)
    whole = (part_ref[...] + acc_ref[...] / mie_ref[...]) * scale
    dirs, half, pair = out_ref.shape
    share = pair // 2
    for r in range(dirs):
        block = whole[:, r * share : (r + 1) * share]
        out_ref[r] = jnp.concatenate([block[:half], block[half:]], axis=1)


def add_shares(in_ref, out_ref):
    summed = jnp.sum(in_ref[...], axis=0)
    share = summed.shape[1] // 2
    out_ref[...] = jnp.concatenate([summed[:, :share], summed[:, share:]], axis=0)


def params(mib):
    return pltpu.CompilerParams(vmem_limit_bytes=mib * MIB)


def cost(flops, mib):
    return pl.CostEstimate(flops=int(flops), bytes_accessed=mib * MIB, transcendentals=0)


def body(incident, cotangent, mie, trans, send_rows, partner_slot):
    count_p, count_n, width = incident.shape
    classes = trans.shape[0]
    peers = lax.axis_size("dom")
    dirs = lax.axis_size("dir")
    cap = send_rows.shape[2]
    remote_rows = peers * cap
    total = count_p * count_n
    chunks = len(SPLITS) - 1
    row_ops = count_p * count_n * width

    rows = jnp.transpose(send_rows[0])
    slots = jnp.transpose(partner_slot)

    def pack(h):
        share = SPLITS[h + 1] - SPLITS[h]
        block = (peers, share, count_n, width)
        return pl.pallas_call(
            functools.partial(pack_rows, SPLITS[h]),
            out_shape=jax.ShapeDtypeStruct(block, BF16),
            in_specs=[smem(), hbm(), hbm()],
            out_specs=hbm(),
            scratch_shapes=[
                pltpu.VMEM((count_p, width), F32),
                pltpu.VMEM((count_p, count_n, width), BF16),
                pltpu.VMEM(block, BF16),
                pltpu.SemaphoreType.DMA((2,)),
                pltpu.SemaphoreType.DMA((4,)),
            ],
            compiler_params=params(8),
            cost_estimate=cost(row_ops, 4),
            name="pack_rows",
        )(rows, mie, incident)

    def send(x):
        return lax.all_to_all(x, "dom", split_axis=0, concat_axis=0, tiled=True)

    stride = count_p + TILE
    field, back, part, order, count = pl.pallas_call(
        functools.partial(local_part, cap),
        out_shape=(
            jax.ShapeDtypeStruct((total, width), F32),
            jax.ShapeDtypeStruct((remote_rows + 1, count_n, width), BF16),
            jax.ShapeDtypeStruct((count_p, width), F32),
            jax.ShapeDtypeStruct((chunks * classes * stride,), jnp.int32),
            jax.ShapeDtypeStruct((chunks * classes,), jnp.int32),
        ),
        in_specs=[smem(), vmem(), vmem(), vmem(), vmem()],
        out_specs=(vmem(), vmem(), vmem(), smem(), smem()),
        scratch_shapes=[
            pltpu.VMEM((count_p + 1, count_n, width), BF16),
            pltpu.VMEM((total, width), BF16),
            pltpu.VMEM((total, width), BF16),
            pltpu.VMEM((total, width), F32),
            pltpu.VMEM((count_p + 1, count_n, width), F32),
        ],
        compiler_params=params(26),
        cost_estimate=cost(4 * classes * row_ops * width, 16),
        name="local_part",
    )(slots, incident, cotangent, mie, trans)

    term = None
    for h in range(chunks):
        last = h == chunks - 1
        share = SPLITS[h + 1] - SPLITS[h]
        packed = pack(h)
        if h > 0:
            packed, part = lax.optimization_barrier((packed, part))
        arrived = send(packed).reshape(peers * share, count_n, width)
        term_shape = jax.ShapeDtypeStruct((peers, cap, width), F32)
        if last:
            out_shape = (
                jax.ShapeDtypeStruct((count_p, count_n, width), BF16),
                jax.ShapeDtypeStruct((count_p, width), F32),
                term_shape,
            )
            extra = (cotangent, mie, part, term)
        else:
            out_shape = (jax.ShapeDtypeStruct((total, width), F32), term_shape)
            extra = ()
        results = pl.pallas_call(
            functools.partial(remote_part, classes, h, cap),
            out_shape=out_shape,
            in_specs=[smem(), smem()] + [vmem()] * (4 + len(extra)),
            out_specs=(vmem(),) * len(out_shape),
            scratch_shapes=[
                pltpu.VMEM((total + count_n, width), F32),
                pltpu.VMEM((TILE * count_n, width), BF16),
            ],
            compiler_params=params(24),
            cost_estimate=cost(2 * peers * share * count_n * width * width, 14),
            name="remote_part",
        )(order, count, arrived, back, field, trans, *extra)
        if last:
            amplitude, part, term = results
        else:
            field, term = results

    term = send(term)
    mine = pl.pallas_call(
        functools.partial(combine, 1.0 / (count_n * dirs)),
        out_shape=jax.ShapeDtypeStruct((dirs, count_p // 2, 2 * width // dirs), F32),
        in_specs=[smem()] + [vmem()] * 3,
        out_specs=vmem(),
        scratch_shapes=[pltpu.VMEM((count_p, width), F32)],
        compiler_params=params(8),
        cost_estimate=cost(row_ops, 1),
        name="combine",
    )(rows, mie, part, term)
    shares = lax.all_to_all(mine, "dir", split_axis=0, concat_axis=0, tiled=True)
    gradient = pl.pallas_call(
        add_shares,
        out_shape=jax.ShapeDtypeStruct((count_p, width // dirs), F32),
        in_specs=[vmem()],
        out_specs=vmem(),
        compiler_params=params(8),
        cost_estimate=cost(row_ops, 1),
        name="add_shares",
    )(shares)
    return amplitude, gradient


def solution(mesh):
    placed = (
        P("dom", "dir", None),
        P("dom", "dir", None),
        P("dom", None),
        P(),
        P("dom", None, None),
        P("dom", None),
    )
    return jax.shard_map(
        body,
        mesh=mesh,
        in_specs=placed,
        out_specs=(P("dom", "dir", None), P("dom", "dir")),
        check_vma=False,
    )
```

```python
import functools

import jax
import jax.numpy as jnp
from jax import lax
from jax.experimental import pallas as pl
from jax.experimental.pallas import tpu as pltpu
from jax.sharding import PartitionSpec as P

TILE = 24
WINDOW = 3
LANES = 128
PARTS = 8
F32 = jnp.float32
BF16 = jnp.bfloat16
MIB = 1 << 20


def vmem():
    return pl.BlockSpec(memory_space=pltpu.VMEM)


def smem():
    return pl.BlockSpec(memory_space=pltpu.SMEM)


def hbm():
    return pl.BlockSpec(memory_space=pl.ANY)


def pack_rows(
    rows_hbm, mie_hbm, inc_hbm, out_hbm, rows_ref, mie_ref, inc_ref, start_ref, out_ref, in_sem, out_sem
):
    peers, cap = out_ref.shape[:2]
    part_peers = peers // PARTS
    gets = [
        pltpu.make_async_copy(inc_hbm, inc_ref, in_sem.at[0]),
        pltpu.make_async_copy(mie_hbm, mie_ref, in_sem.at[1]),
        pltpu.make_async_copy(rows_hbm, rows_ref, in_sem.at[2]),
    ]
    for get in gets:
        get.start()
    for get in gets:
        get.wait()

    def scale(p, carry):
        start_ref[p] = (mie_ref[pl.ds(p, 1), :] * inc_ref[p].astype(F32)).astype(BF16)
        return carry

    lax.fori_loop(0, inc_ref.shape[0], scale, 0, unroll=8)

    def put(part):
        here = pl.ds(part * part_peers, part_peers)
        return pltpu.make_async_copy(out_ref.at[here], out_hbm.at[here], out_sem.at[part])

    for part in range(PARTS):
        for i in range(part_peers):
            peer = part * part_peers + i
            for c in range(cap):
                out_ref[peer, c] = start_ref[rows_ref[c, peer]]
        put(part).start()
    for part in range(PARTS):
        put(part).wait()


def local_part(
    slot_ref,
    rows_ref,
    inc_hbm,
    cot_hbm,
    mie_hbm,
    trans_hbm,
    field_ref,
    back_ref,
    grad_ref,
    owner_ref,
    order_ref,
    count_ref,
    inc_ref,
    cot_ref,
    mie_ref,
    trans_ref,
    start_ref,
    adj_ref,
    lhs_ref,
    prod_ref,
    adjoint_ref,
    in_sem,
    trans_sem,
):
    count_p, count_n, width = inc_ref.shape
    classes = slot_ref.shape[0]
    stride = count_p + TILE
    dummy = back_ref.shape[0] - 1
    gets = [
        pltpu.make_async_copy(mie_hbm, mie_ref, in_sem.at[0]),
        pltpu.make_async_copy(inc_hbm, inc_ref, in_sem.at[1]),
        pltpu.make_async_copy(cot_hbm, cot_ref, in_sem.at[2]),
    ]

    def get_trans(k):
        return pltpu.make_async_copy(trans_hbm.at[k], trans_ref.at[k], trans_sem.at[k])

    for get in gets:
        get.start()
    for k in range(classes):
        get_trans(k).start()
    for get in gets:
        get.wait()

    def prepare(p, carry):
        scale = mie_ref[pl.ds(p, 1), :]
        inc = inc_ref[p].astype(F32)
        start_ref[p] = (scale * inc).astype(BF16)
        at = pl.multiple_of(p * count_n, count_n)
        adj_ref[pl.ds(at, count_n), :] = (scale * cot_ref[p].astype(F32)).astype(BF16)
        field_ref[pl.ds(at, count_n), :] = inc
        adjoint_ref[p] = jnp.zeros((count_n, width), F32)
        return carry

    lax.fori_loop(0, count_p, prepare, 0, unroll=4)
    start_ref[count_p] = jnp.zeros((count_n, width), BF16)
    adjoint_ref[count_p] = jnp.zeros((count_n, width), F32)

    def one_class(k, carry):
        base = k * stride

        def pick(p, tally):
            slot = slot_ref[k, p]
            is_local = (slot >= 0) & (slot < count_p)
            source = jnp.where(is_local, slot, count_p)
            at = pl.multiple_of(p * count_n, count_n)
            lhs_ref[pl.ds(at, count_n), :] = start_ref[source]
            remote = slot - count_p
            order_ref[base + tally] = remote * 128 + p
            return tally + (remote >= 0).astype(jnp.int32)

        tally = lax.fori_loop(0, count_p, pick, jnp.int32(0), unroll=4)
        count_ref[k] = tally
        for extra in range(TILE):
            order_ref[base + tally + extra] = count_p
        get_trans(k).wait()
        field_ref[...] += jnp.dot(lhs_ref[...], trans_ref[k], preferred_element_type=F32)
        prod_ref[...] = lax.dot_general(
            adj_ref[...],
            trans_ref[k],
            (((1,), (1,)), ((), ())),
            preferred_element_type=F32,
        )

        def spread(p, c):
            slot = slot_ref[k, p]
            is_local = (slot >= 0) & (slot < count_p)
            at = pl.multiple_of(p * count_n, count_n)
            prod = prod_ref[pl.ds(at, count_n), :]
            back_ref[jnp.where(slot >= count_p, slot - count_p, dummy)] = prod.astype(BF16)
            adjoint_ref[jnp.where(is_local, slot, count_p)] += prod
            return c

        lax.fori_loop(0, count_p, spread, 0, unroll=4)
        return carry

    lax.fori_loop(0, classes, one_class, 0)

    def own(q, carry):
        lane = lax.broadcasted_iota(jnp.int32, (1, LANES), 1)
        for c in range(rows_ref.shape[0]):
            owner_ref[pl.ds(q * rows_ref.shape[0] + c, 1), :] = (lane == rows_ref[c, q]).astype(F32)
        return carry

    lax.fori_loop(0, rows_ref.shape[1], own, 0)

    def finish(p, carry):
        at = pl.multiple_of(p * count_n, count_n)
        both = inc_ref[p].astype(F32) * adjoint_ref[p]
        both += cot_ref[p].astype(F32) * field_ref[pl.ds(at, count_n), :]
        grad_ref[pl.ds(p, 1), :] = jnp.sum(both, axis=0, keepdims=True)
        return carry

    lax.fori_loop(0, count_p, finish, 0, unroll=4)


def remote_terms(arrived_hbm, back_hbm, term_ref, arrived_ref, back_ref, sem):
    peers, cap = term_ref.shape[:2]
    part_peers = peers // PARTS

    def get(part):
        here = pl.ds(part * part_peers * cap, part_peers * cap)
        return (
            pltpu.make_async_copy(arrived_hbm.at[here], arrived_ref.at[here], sem.at[0, part]),
            pltpu.make_async_copy(back_hbm.at[here], back_ref.at[here], sem.at[1, part]),
        )

    for part in range(PARTS):
        for copy in get(part):
            copy.start()
    for part in range(PARTS):
        for copy in get(part):
            copy.wait()

        def one(i, carry, part=part):
            peer = part * part_peers + i
            here = pl.ds(peer * cap, cap)
            both = arrived_ref[here].astype(F32) * back_ref[here].astype(F32)
            term_ref[peer] = jnp.sum(both, axis=1).astype(BF16)
            return carry

        lax.fori_loop(0, part_peers, one, 0)


def remote_field(
    order_ref,
    count_ref,
    arrived_hbm,
    trans_hbm,
    cot_hbm,
    part_hbm,
    acc_ref,
    grad_hbm,
    arrived_ref,
    trans_ref,
    cot_ref,
    part_ref,
    grad_ref,
    lhs_even,
    lhs_odd,
    moved_even,
    moved_odd,
    in_sem,
    trans_sem,
    out_sem,
):
    classes = trans_ref.shape[0]
    count_p, count_n, width = cot_ref.shape
    stride = count_p + TILE
    get_arrived = pltpu.make_async_copy(arrived_hbm, arrived_ref, in_sem.at[0])
    late = [
        pltpu.make_async_copy(cot_hbm, cot_ref, in_sem.at[1]),
        pltpu.make_async_copy(part_hbm, part_ref, in_sem.at[2]),
    ]

    def get_trans(k):
        return pltpu.make_async_copy(trans_hbm.at[k], trans_ref.at[k], trans_sem.at[k])

    get_arrived.start()
    for k in range(WINDOW):
        get_trans(k).start()

    def clear(p, carry):
        at = pl.multiple_of(p * count_n, count_n)
        acc_ref[pl.ds(at, count_n), :] = jnp.zeros((count_n, width), F32)
        return carry

    lax.fori_loop(0, count_p + 1, clear, 0, unroll=5)
    moved_odd[...] = jnp.zeros_like(moved_odd)
    get_arrived.wait()

    def gather(k, lhs, t=0):
        base = k * stride + t * TILE
        for i in range(TILE):
            source = lax.shift_right_logical(order_ref[base + i], 7)
            lhs[pl.ds(i * count_n, count_n), :] = arrived_ref[source]

    def scatter(k, moved, t=0):
        base = k * stride + t * TILE
        for i in range(TILE):
            p = order_ref[base + i] & 127
            at = pl.multiple_of(p * count_n, count_n)
            acc_ref[pl.ds(at, count_n), :] += moved[pl.ds(i * count_n, count_n), :]

    def fetch(k):
        get_trans(k).wait()

        @pl.when(k + WINDOW < classes)
        def _():
            get_trans(k + WINDOW).start()

        @pl.when(k + WINDOW == classes)
        def _():
            for get in late:
                get.start()

    gather(0, lhs_even)

    def two_classes(i, carry):
        k = 2 * i
        fetch(k)
        moved_even[...] = jnp.dot(lhs_even[...], trans_ref[k], preferred_element_type=F32)
        gather(k + 1, lhs_odd)
        scatter(jnp.maximum(k - 1, 0), moved_odd)
        fetch(k + 1)
        moved_odd[...] = jnp.dot(lhs_odd[...], trans_ref[k + 1], preferred_element_type=F32)
        gather(jnp.minimum(k + 2, classes - 1), lhs_even)
        scatter(k, moved_even)
        return carry

    lax.fori_loop(0, classes // 2, two_classes, 0)
    scatter(classes - 1, moved_odd)

    def more(k, carry):
        def one_tile(t, c):
            gather(k, lhs_even, t)
            moved_even[...] = jnp.dot(lhs_even[...], trans_ref[k], preferred_element_type=F32)
            scatter(k, moved_even, t)
            return c

        lax.fori_loop(1, lax.div(count_ref[k] + (TILE - 1), TILE), one_tile, 0)
        return carry

    lax.fori_loop(0, classes, more, 0)
    for get in late:
        get.wait()

    def finish(p, carry):
        at = pl.multiple_of(p * count_n, count_n)
        grad_ref[pl.ds(p, 1), :] = part_ref[pl.ds(p, 1), :] + jnp.sum(
            cot_ref[p].astype(F32) * acc_ref[pl.ds(at, count_n), :], axis=0, keepdims=True
        )
        return carry

    lax.fori_loop(0, count_p, finish, 0, unroll=4)
    put = pltpu.make_async_copy(grad_ref, grad_hbm, out_sem)
    put.start()
    put.wait()


def amplitudes(acc_ref, field_hbm, mie_hbm, amp_hbm, field_ref, mie_ref, amp_ref, in_sem, out_sem):
    count_p, count_n, width = amp_ref.shape
    step = count_p // PARTS

    def get(part):
        here = pl.ds(part * step * count_n, step * count_n)
        return pltpu.make_async_copy(field_hbm.at[here], field_ref.at[here], in_sem.at[part])

    def put(part):
        here = pl.ds(part * step, step)
        return pltpu.make_async_copy(amp_ref.at[here], amp_hbm.at[here], out_sem.at[part])

    get_mie = pltpu.make_async_copy(mie_hbm, mie_ref, in_sem.at[PARTS])
    get_mie.start()
    for part in range(PARTS):
        get(part).start()
    get_mie.wait()
    for part in range(PARTS):
        get(part).wait()

        def one(i, carry, part=part):
            p = part * step + i
            here = pl.ds(pl.multiple_of(p * count_n, count_n), count_n)
            field = field_ref[here, :] + acc_ref[here, :]
            amp_ref[p] = (mie_ref[pl.ds(p, 1), :] * field).astype(BF16)
            return carry

        lax.fori_loop(0, step, one, 0, unroll=4)
        put(part).start()
    for part in range(PARTS):
        put(part).wait()


def combine(scale, owner_hbm, mie_hbm, part_hbm, term_ref, out_ref, owner_ref, mie_ref, part_ref, sem):
    gets = [
        pltpu.make_async_copy(owner_hbm, owner_ref, sem.at[0]),
        pltpu.make_async_copy(mie_hbm, mie_ref, sem.at[1]),
        pltpu.make_async_copy(part_hbm, part_ref, sem.at[2]),
    ]
    for get in gets:
        get.start()
    for get in gets:
        get.wait()
    count_p, width = mie_ref.shape
    mine = lax.dot_general(
        owner_ref[...].astype(BF16),
        term_ref[...].reshape(owner_ref.shape[0], width),
        (((0,), (0,)), ((), ())),
        preferred_element_type=F32,
    )
    whole = (part_ref[...] + mine[:count_p] / mie_ref[...]) * scale
    dirs, half, pair = out_ref.shape
    share = pair // 2
    for r in range(dirs):
        block = whole[:, r * share : (r + 1) * share]
        out_ref[r] = jnp.concatenate([block[:half], block[half:]], axis=1)


def add_shares(in_ref, out_ref):
    summed = jnp.sum(in_ref[...], axis=0)
    share = summed.shape[1] // 2
    out_ref[...] = jnp.concatenate([summed[:, :share], summed[:, share:]], axis=0)


def params(mib=60):
    return pltpu.CompilerParams(vmem_limit_bytes=mib * MIB)


def cost(flops, mib):
    return pl.CostEstimate(flops=int(flops), bytes_accessed=mib * MIB, transcendentals=0)


def stay(x):
    return pltpu.with_memory_space_constraint(x, pltpu.VMEM)


def body(incident, cotangent, mie, trans, send_rows, partner_slot):
    count_p, count_n, width = incident.shape
    classes = trans.shape[0]
    peers = lax.axis_size("dom")
    dirs = lax.axis_size("dir")
    cap = send_rows.shape[2]
    remote_rows = peers * cap
    total = count_p * count_n
    row_ops = count_p * count_n * width

    rows = jnp.transpose(send_rows[0])
    slots = jnp.transpose(partner_slot)

    def send(x):
        return lax.all_to_all(x, "dom", split_axis=0, concat_axis=0, tiled=True)

    packed = pl.pallas_call(
        pack_rows,
        out_shape=jax.ShapeDtypeStruct((peers, cap, count_n, width), BF16),
        in_specs=[hbm()] * 3,
        out_specs=hbm(),
        scratch_shapes=[
            pltpu.SMEM((cap, peers), jnp.int32),
            pltpu.VMEM((count_p, width), F32),
            pltpu.VMEM((count_p, count_n, width), BF16),
            pltpu.VMEM((count_p, count_n, width), BF16),
            pltpu.VMEM((peers, cap, count_n, width), BF16),
            pltpu.SemaphoreType.DMA((3,)),
            pltpu.SemaphoreType.DMA((PARTS,)),
        ],
        compiler_params=params(),
        cost_estimate=cost(row_ops, 4),
        name="pack_rows",
    )(rows, mie, incident)
    arrived = send(packed).reshape(remote_rows, count_n, width)

    field, back, part, owner, order, count = pl.pallas_call(
        local_part,
        out_shape=(
            jax.ShapeDtypeStruct((total, width), F32),
            jax.ShapeDtypeStruct((remote_rows + 1, count_n, width), BF16),
            jax.ShapeDtypeStruct((count_p, width), F32),
            jax.ShapeDtypeStruct((remote_rows, LANES), F32),
            jax.ShapeDtypeStruct((classes * (count_p + TILE),), jnp.int32),
            jax.ShapeDtypeStruct((classes,), jnp.int32),
        ),
        in_specs=[smem(), smem()] + [hbm()] * 4,
        out_specs=(vmem(),) * 4 + (smem(),) * 2,
        scratch_shapes=[
            pltpu.VMEM((count_p, count_n, width), BF16),
            pltpu.VMEM((count_p, count_n, width), BF16),
            pltpu.VMEM((count_p, width), F32),
            pltpu.VMEM((classes, width, width), BF16),
            pltpu.VMEM((count_p + 1, count_n, width), BF16),
            pltpu.VMEM((total, width), BF16),
            pltpu.VMEM((total, width), BF16),
            pltpu.VMEM((total, width), F32),
            pltpu.VMEM((count_p + 1, count_n, width), F32),
            pltpu.SemaphoreType.DMA((3,)),
            pltpu.SemaphoreType.DMA((classes,)),
        ],
        compiler_params=params(),
        cost_estimate=cost(4 * classes * row_ops * width, 16),
        name="local_part",
    )(slots, rows, incident, cotangent, mie, trans)

    term = pl.pallas_call(
        remote_terms,
        out_shape=jax.ShapeDtypeStruct((peers, cap, width), BF16),
        in_specs=[hbm(), hbm()],
        out_specs=vmem(),
        scratch_shapes=[
            pltpu.VMEM((remote_rows, count_n, width), BF16),
            pltpu.VMEM((remote_rows, count_n, width), BF16),
            pltpu.SemaphoreType.DMA((2, PARTS)),
        ],
        compiler_params=params(),
        cost_estimate=cost(4 * row_ops, 8),
        name="remote_terms",
    )(arrived, back)
    term = send(term)

    acc, part = pl.pallas_call(
        remote_field,
        out_shape=(
            pltpu.VMEM((total + count_n, width), F32),
            jax.ShapeDtypeStruct((count_p, width), F32),
        ),
        in_specs=[smem(), smem()] + [hbm()] * 4,
        out_specs=(vmem(), hbm()),
        scratch_shapes=[
            pltpu.VMEM((remote_rows, count_n, width), BF16),
            pltpu.VMEM((classes, width, width), BF16),
            pltpu.VMEM((count_p, count_n, width), BF16),
            pltpu.VMEM((count_p, width), F32),
            pltpu.VMEM((count_p, width), F32),
            pltpu.VMEM((TILE * count_n, width), BF16),
            pltpu.VMEM((TILE * count_n, width), BF16),
            pltpu.VMEM((TILE * count_n, width), F32),
            pltpu.VMEM((TILE * count_n, width), F32),
            pltpu.SemaphoreType.DMA((3,)),
            pltpu.SemaphoreType.DMA((classes,)),
            pltpu.SemaphoreType.DMA,
        ],
        compiler_params=params(56),
        cost_estimate=cost(2 * remote_rows * count_n * width * width, 14),
        name="remote_field",
    )(order, count, arrived, trans, cotangent, part)
    acc = stay(acc)

    mine = pl.pallas_call(
        functools.partial(combine, 1.0 / (count_n * dirs)),
        out_shape=jax.ShapeDtypeStruct((dirs, count_p // 2, 2 * width // dirs), F32),
        in_specs=[hbm()] * 3 + [vmem()],
        out_specs=vmem(),
        scratch_shapes=[
            pltpu.VMEM((remote_rows, LANES), F32),
            pltpu.VMEM((count_p, width), F32),
            pltpu.VMEM((count_p, width), F32),
            pltpu.SemaphoreType.DMA((3,)),
        ],
        compiler_params=params(24),
        cost_estimate=cost(row_ops, 1),
        name="combine",
    )(owner, mie, part, term)
    mine, field = lax.optimization_barrier((mine, field))
    amplitude = pl.pallas_call(
        amplitudes,
        out_shape=jax.ShapeDtypeStruct((count_p, count_n, width), BF16),
        in_specs=[vmem(), hbm(), hbm()],
        out_specs=hbm(),
        scratch_shapes=[
            pltpu.VMEM((total, width), F32),
            pltpu.VMEM((count_p, width), F32),
            pltpu.VMEM((count_p, count_n, width), BF16),
            pltpu.SemaphoreType.DMA((PARTS + 1,)),
            pltpu.SemaphoreType.DMA((PARTS,)),
        ],
        compiler_params=params(56),
        cost_estimate=cost(row_ops, 5),
        name="amplitudes",
    )(acc, field, mie)
    shares = lax.all_to_all(mine, "dir", split_axis=0, concat_axis=0, tiled=True)
    gradient = pl.pallas_call(
        add_shares,
        out_shape=jax.ShapeDtypeStruct((count_p, width // dirs), F32),
        in_specs=[vmem()],
        out_specs=vmem(),
        compiler_params=params(8),
        cost_estimate=cost(row_ops, 1),
        name="add_shares",
    )(shares)
    return amplitude, gradient


def solution(mesh):
    placed = (
        P("dom", "dir", None),
        P("dom", "dir", None),
        P("dom", None),
        P(),
        P("dom", None, None),
        P("dom", None),
    )
    return jax.shard_map(
        body,
        mesh=mesh,
        in_specs=placed,
        out_specs=(P("dom", "dir", None), P("dom", "dir")),
        check_vma=False,
    )
```

```python
import functools

import jax
import jax.numpy as jnp
from jax import lax
from jax.experimental import pallas as pl
from jax.experimental.pallas import tpu as pltpu
from jax.sharding import PartitionSpec as P

TILE = 32
WINDOW = 3
LANES = 128
NEAR = 128
SIZES = (16, 24, 32)
PARTS = 8
F32 = jnp.float32
BF16 = jnp.bfloat16
MIB = 1 << 20


def vmem():
    return pl.BlockSpec(memory_space=pltpu.VMEM)


def smem():
    return pl.BlockSpec(memory_space=pltpu.SMEM)


def hbm():
    return pl.BlockSpec(memory_space=pl.ANY)


def pack_rows(
    rows_hbm, mie_hbm, inc_hbm, out_hbm, rows_ref, mie_ref, inc_ref, start_ref, out_ref, in_sem, out_sem
):
    peers, cap = out_ref.shape[:2]
    part_peers = peers // PARTS
    pieces = in_sem.shape[0] - 2
    step = inc_ref.shape[0] // pieces

    def get(piece):
        here = pl.ds(piece * step, step)
        return pltpu.make_async_copy(inc_hbm.at[here], inc_ref.at[here], in_sem.at[piece])

    get_mie = pltpu.make_async_copy(mie_hbm, mie_ref, in_sem.at[pieces])
    get_rows = pltpu.make_async_copy(rows_hbm, rows_ref, in_sem.at[pieces + 1])
    get_mie.start()
    for piece in range(pieces):
        get(piece).start()
    get_rows.start()
    get_mie.wait()
    for piece in range(pieces):
        get(piece).wait()

        def scale(i, carry, piece=piece):
            p = piece * step + i
            start_ref[p] = (mie_ref[pl.ds(p, 1), :] * inc_ref[p].astype(F32)).astype(BF16)
            return carry

        lax.fori_loop(0, step, scale, 0, unroll=8)
    get_rows.wait()

    def put(part):
        here = pl.ds(part * part_peers, part_peers)
        return pltpu.make_async_copy(out_ref.at[here], out_hbm.at[here], out_sem.at[part])

    for part in range(PARTS):
        for i in range(part_peers):
            peer = part * part_peers + i
            for c in range(cap):
                out_ref[peer, c] = start_ref[rows_ref[c, peer]]
        put(part).start()
    for part in range(PARTS):
        put(part).wait()


def local_part(
    slot_ref,
    rows_ref,
    inc_hbm,
    cot_hbm,
    mie_hbm,
    trans_hbm,
    field_ref,
    near_ref,
    far_hbm,
    grad_ref,
    owner_ref,
    order_ref,
    count_ref,
    inc_ref,
    cot_ref,
    mie_ref,
    trans_ref,
    start_ref,
    adj_ref,
    lhs_ref,
    prod_ref,
    adjoint_ref,
    back_ref,
    in_sem,
    trans_sem,
    far_sem,
):
    count_p, count_n, width = inc_ref.shape
    classes = slot_ref.shape[0]
    stride = count_p + TILE
    dummy = back_ref.shape[0] - 1
    gets = [
        pltpu.make_async_copy(mie_hbm, mie_ref, in_sem.at[0]),
        pltpu.make_async_copy(inc_hbm, inc_ref, in_sem.at[1]),
        pltpu.make_async_copy(cot_hbm, cot_ref, in_sem.at[2]),
    ]

    def get_trans(k):
        return pltpu.make_async_copy(trans_hbm.at[k], trans_ref.at[k], trans_sem.at[k])

    for get in gets:
        get.start()
    for k in range(classes):
        get_trans(k).start()
    for get in gets:
        get.wait()

    def prepare(p, carry):
        scale = mie_ref[pl.ds(p, 1), :]
        inc = inc_ref[p].astype(F32)
        start_ref[p] = (scale * inc).astype(BF16)
        at = pl.multiple_of(p * count_n, count_n)
        adj_ref[pl.ds(at, count_n), :] = (scale * cot_ref[p].astype(F32)).astype(BF16)
        field_ref[pl.ds(at, count_n), :] = inc
        adjoint_ref[p] = jnp.zeros((count_n, width), F32)
        return carry

    lax.fori_loop(0, count_p, prepare, 0, unroll=4)
    start_ref[count_p] = jnp.zeros((count_n, width), BF16)
    adjoint_ref[count_p] = jnp.zeros((count_n, width), F32)

    def one_class(k, carry):
        base = k * stride

        def pick(p, tally):
            slot = slot_ref[k, p]
            is_local = (slot >= 0) & (slot < count_p)
            source = jnp.where(is_local, slot, count_p)
            at = pl.multiple_of(p * count_n, count_n)
            lhs_ref[pl.ds(at, count_n), :] = start_ref[source]
            remote = slot - count_p
            order_ref[base + tally] = remote * 128 + p
            return tally + (remote >= 0).astype(jnp.int32)

        tally = lax.fori_loop(0, count_p, pick, jnp.int32(0), unroll=4)
        count_ref[k] = tally
        for extra in range(TILE):
            order_ref[base + tally + extra] = count_p
        get_trans(k).wait()
        field_ref[...] += jnp.dot(lhs_ref[...], trans_ref[k], preferred_element_type=F32)
        prod_ref[...] = lax.dot_general(
            adj_ref[...],
            trans_ref[k],
            (((1,), (1,)), ((), ())),
            preferred_element_type=F32,
        )

        def spread(p, c):
            slot = slot_ref[k, p]
            is_local = (slot >= 0) & (slot < count_p)
            at = pl.multiple_of(p * count_n, count_n)
            prod = prod_ref[pl.ds(at, count_n), :]
            back_ref[jnp.where(slot >= count_p, slot - count_p, dummy)] = prod.astype(BF16)
            adjoint_ref[jnp.where(is_local, slot, count_p)] += prod
            return c

        lax.fori_loop(0, count_p, spread, 0, unroll=4)
        return carry

    lax.fori_loop(0, classes, one_class, 0)

    put_far = pltpu.make_async_copy(back_ref.at[pl.ds(NEAR, dummy - NEAR)], far_hbm, far_sem)
    put_far.start()

    def keep(i, carry):
        near_ref[i] = back_ref[i]
        return carry

    lax.fori_loop(0, NEAR, keep, 0, unroll=4)

    def own(q, carry):
        lane = lax.broadcasted_iota(jnp.int32, (1, LANES), 1)
        for c in range(rows_ref.shape[0]):
            owner_ref[pl.ds(q * rows_ref.shape[0] + c, 1), :] = (lane == rows_ref[c, q]).astype(F32)
        return carry

    lax.fori_loop(0, rows_ref.shape[1], own, 0)

    def finish(p, carry):
        at = pl.multiple_of(p * count_n, count_n)
        both = inc_ref[p].astype(F32) * adjoint_ref[p]
        both += cot_ref[p].astype(F32) * field_ref[pl.ds(at, count_n), :]
        grad_ref[pl.ds(p, 1), :] = jnp.sum(both, axis=0, keepdims=True)
        return carry

    lax.fori_loop(0, count_p, finish, 0, unroll=4)
    put_far.wait()


def remote_terms(arrived_hbm, far_hbm, back_ref, term_ref, near_ref, last_ref, far_ref, sem):
    peers, cap = term_ref.shape[:2]
    rows_in = peers * cap
    step = rows_in // PARTS
    parts_near = NEAR // step

    def get(part):
        start = part * step
        here = pl.ds(start, step)
        if part < parts_near:
            return [pltpu.make_async_copy(arrived_hbm.at[here], near_ref.at[here], sem.at[0, part])]
        there = pl.ds(start - NEAR, step)
        return [
            pltpu.make_async_copy(arrived_hbm.at[here], last_ref.at[there], sem.at[0, part]),
            pltpu.make_async_copy(far_hbm.at[there], far_ref.at[there], sem.at[1, part]),
        ]

    for part in range(PARTS):
        for copy in get(part):
            copy.start()
    for part in range(PARTS):
        for copy in get(part):
            copy.wait()
        is_near = part < parts_near
        got_ref, kept_ref = (near_ref, back_ref) if is_near else (last_ref, far_ref)
        base = part * step - (0 if is_near else NEAR)

        def one(i, carry, part=part, got_ref=got_ref, kept_ref=kept_ref, base=base):
            here = pl.ds(base + i * cap, cap)
            both = got_ref[here].astype(F32) * kept_ref[here].astype(F32)
            term_ref[part * (step // cap) + i] = jnp.sum(both, axis=1).astype(BF16)
            return carry

        lax.fori_loop(0, step // cap, one, 0)


def remote_field(
    order_ref,
    count_ref,
    arrived_hbm,
    trans_hbm,
    cot_hbm,
    part_hbm,
    acc_ref,
    grad_hbm,
    arrived_ref,
    trans_ref,
    cot_ref,
    part_ref,
    grad_ref,
    lhs_ref,
    moved_ref,
    in_sem,
    trans_sem,
    out_sem,
):
    classes = trans_ref.shape[0]
    count_p, count_n, width = cot_ref.shape
    stride = count_p + TILE
    get_arrived = pltpu.make_async_copy(arrived_hbm, arrived_ref, in_sem.at[0])
    late = [
        pltpu.make_async_copy(cot_hbm, cot_ref, in_sem.at[1]),
        pltpu.make_async_copy(part_hbm, part_ref, in_sem.at[2]),
    ]

    def get_trans(k):
        return pltpu.make_async_copy(trans_hbm.at[k], trans_ref.at[k], trans_sem.at[k])

    get_arrived.start()
    for k in range(WINDOW):
        get_trans(k).start()

    def clear(p, carry):
        at = pl.multiple_of(p * count_n, count_n)
        acc_ref[pl.ds(at, count_n), :] = jnp.zeros((count_n, width), F32)
        return carry

    lax.fori_loop(0, count_p + 1, clear, 0, unroll=5)
    get_arrived.wait()

    def tile(k, first, size):
        base = k * stride + first
        for i in range(size):
            source = lax.shift_right_logical(order_ref[base + i], 7)
            lhs_ref[pl.ds(i * count_n, count_n), :] = arrived_ref[source]
        rows = pl.ds(0, size * count_n)
        moved_ref[rows, :] = jnp.dot(lhs_ref[rows, :], trans_ref[k], preferred_element_type=F32)
        for i in range(size):
            p = order_ref[base + i] & 127
            at = pl.multiple_of(p * count_n, count_n)
            acc_ref[pl.ds(at, count_n), :] += moved_ref[pl.ds(i * count_n, count_n), :]

    def fetch(k):
        get_trans(k).wait()

        @pl.when(k + WINDOW < classes)
        def _():
            get_trans(k + WINDOW).start()

        @pl.when(k + WINDOW == classes)
        def _():
            for get in late:
                get.start()

    def one_class(k, carry):
        fetch(k)
        count = count_ref[k]
        for low, size in zip((-1,) + SIZES, SIZES):
            here = count > low
            if size < TILE:
                here = here & (count <= size)

            @pl.when(here)
            def _(size=size):
                tile(k, 0, size)

        def more(t, c):
            tile(k, t * TILE, TILE)
            return c

        lax.fori_loop(1, lax.div(count + (TILE - 1), TILE), more, 0)
        return carry

    lax.fori_loop(0, classes, one_class, 0)
    for get in late:
        get.wait()

    def finish(p, carry):
        at = pl.multiple_of(p * count_n, count_n)
        grad_ref[pl.ds(p, 1), :] = part_ref[pl.ds(p, 1), :] + jnp.sum(
            cot_ref[p].astype(F32) * acc_ref[pl.ds(at, count_n), :], axis=0, keepdims=True
        )
        return carry

    lax.fori_loop(0, count_p, finish, 0, unroll=4)
    put = pltpu.make_async_copy(grad_ref, grad_hbm, out_sem)
    put.start()
    put.wait()


def amplitudes(acc_ref, field_hbm, mie_hbm, amp_hbm, field_ref, mie_ref, amp_ref, in_sem, out_sem):
    count_p, count_n, width = amp_ref.shape
    step = count_p // PARTS

    def get(part):
        here = pl.ds(part * step * count_n, step * count_n)
        return pltpu.make_async_copy(field_hbm.at[here], field_ref.at[here], in_sem.at[part])

    def put(part):
        here = pl.ds(part * step, step)
        return pltpu.make_async_copy(amp_ref.at[here], amp_hbm.at[here], out_sem.at[part])

    get_mie = pltpu.make_async_copy(mie_hbm, mie_ref, in_sem.at[PARTS])
    get_mie.start()
    for part in range(PARTS):
        get(part).start()
    get_mie.wait()
    for part in range(PARTS):
        get(part).wait()

        def one(i, carry, part=part):
            p = part * step + i
            here = pl.ds(pl.multiple_of(p * count_n, count_n), count_n)
            field = field_ref[here, :] + acc_ref[here, :]
            amp_ref[p] = (mie_ref[pl.ds(p, 1), :] * field).astype(BF16)
            return carry

        lax.fori_loop(0, step, one, 0, unroll=4)
        put(part).start()
    for part in range(PARTS):
        put(part).wait()


def combine(scale, owner_hbm, mie_hbm, part_hbm, term_ref, out_ref, owner_ref, mie_ref, part_ref, sem):
    gets = [
        pltpu.make_async_copy(owner_hbm, owner_ref, sem.at[0]),
        pltpu.make_async_copy(mie_hbm, mie_ref, sem.at[1]),
        pltpu.make_async_copy(part_hbm, part_ref, sem.at[2]),
    ]
    for get in gets:
        get.start()
    for get in gets:
        get.wait()
    count_p, width = mie_ref.shape
    mine = lax.dot_general(
        owner_ref[...].astype(BF16),
        term_ref[...].reshape(owner_ref.shape[0], width),
        (((0,), (0,)), ((), ())),
        preferred_element_type=F32,
    )
    whole = (part_ref[...] + mine[:count_p] / mie_ref[...]) * scale
    dirs, half, pair = out_ref.shape
    share = pair // 2
    for r in range(dirs):
        block = whole[:, r * share : (r + 1) * share]
        out_ref[r] = jnp.concatenate([block[:half], block[half:]], axis=1)


def add_shares(in_ref, out_ref):
    summed = jnp.sum(in_ref[...], axis=0)
    share = summed.shape[1] // 2
    out_ref[...] = jnp.concatenate([summed[:, :share], summed[:, share:]], axis=0)


def params(mib=60):
    return pltpu.CompilerParams(vmem_limit_bytes=mib * MIB)


def cost(flops, mib):
    return pl.CostEstimate(flops=int(flops), bytes_accessed=mib * MIB, transcendentals=0)


def stay(x):
    return pltpu.with_memory_space_constraint(x, pltpu.VMEM)


def far_off(x):
    return pltpu.with_memory_space_constraint(x, pltpu.HBM)


def body(incident, cotangent, mie, trans, send_rows, partner_slot):
    count_p, count_n, width = incident.shape
    classes = trans.shape[0]
    peers = lax.axis_size("dom")
    dirs = lax.axis_size("dir")
    cap = send_rows.shape[2]
    remote_rows = peers * cap
    total = count_p * count_n
    row_ops = count_p * count_n * width

    rows = jnp.transpose(send_rows[0])
    slots = jnp.transpose(partner_slot)

    def send(x):
        return lax.all_to_all(x, "dom", split_axis=0, concat_axis=0, tiled=True)

    packed = pl.pallas_call(
        pack_rows,
        out_shape=jax.ShapeDtypeStruct((peers, cap, count_n, width), BF16),
        in_specs=[hbm()] * 3,
        out_specs=hbm(),
        scratch_shapes=[
            pltpu.SMEM((cap, peers), jnp.int32),
            pltpu.VMEM((count_p, width), F32),
            pltpu.VMEM((count_p, count_n, width), BF16),
            pltpu.VMEM((count_p, count_n, width), BF16),
            pltpu.VMEM((peers, cap, count_n, width), BF16),
            pltpu.SemaphoreType.DMA((6,)),
            pltpu.SemaphoreType.DMA((PARTS,)),
        ],
        compiler_params=params(),
        cost_estimate=cost(row_ops, 4),
        name="pack_rows",
    )(rows, mie, incident)
    arrived = send(packed).reshape(remote_rows, count_n, width)

    far_rows = remote_rows - NEAR
    field, near, far, part, owner, order, count = pl.pallas_call(
        local_part,
        out_shape=(
            jax.ShapeDtypeStruct((total, width), F32),
            pltpu.VMEM((NEAR, count_n, width), BF16),
            jax.ShapeDtypeStruct((far_rows, count_n, width), BF16),
            jax.ShapeDtypeStruct((count_p, width), F32),
            jax.ShapeDtypeStruct((remote_rows, LANES), F32),
            jax.ShapeDtypeStruct((classes * (count_p + TILE),), jnp.int32),
            jax.ShapeDtypeStruct((classes,), jnp.int32),
        ),
        in_specs=[smem(), smem()] + [hbm()] * 4,
        out_specs=(vmem(), vmem(), hbm(), vmem(), vmem(), smem(), smem()),
        scratch_shapes=[
            pltpu.VMEM((count_p, count_n, width), BF16),
            pltpu.VMEM((count_p, count_n, width), BF16),
            pltpu.VMEM((count_p, width), F32),
            pltpu.VMEM((classes, width, width), BF16),
            pltpu.VMEM((count_p + 1, count_n, width), BF16),
            pltpu.VMEM((total, width), BF16),
            pltpu.VMEM((total, width), BF16),
            pltpu.VMEM((total, width), F32),
            pltpu.VMEM((count_p + 1, count_n, width), F32),
            pltpu.VMEM((remote_rows + 1, count_n, width), BF16),
            pltpu.SemaphoreType.DMA((3,)),
            pltpu.SemaphoreType.DMA((classes,)),
            pltpu.SemaphoreType.DMA,
        ],
        compiler_params=params(),
        cost_estimate=cost(4 * classes * row_ops * width, 16),
        name="local_part",
    )(slots, rows, incident, cotangent, mie, trans)
    near = stay(near)

    term = pl.pallas_call(
        remote_terms,
        out_shape=jax.ShapeDtypeStruct((peers, cap, width), BF16),
        in_specs=[hbm(), hbm(), vmem()],
        out_specs=vmem(),
        scratch_shapes=[
            pltpu.VMEM((NEAR, count_n, width), BF16),
            pltpu.VMEM((far_rows, count_n, width), BF16),
            pltpu.VMEM((far_rows, count_n, width), BF16),
            pltpu.SemaphoreType.DMA((2, PARTS)),
        ],
        compiler_params=params(58),
        cost_estimate=cost(4 * row_ops, 8),
        name="remote_terms",
    )(arrived, far, near)
    term = send(term)

    acc, part = pl.pallas_call(
        remote_field,
        out_shape=(
            pltpu.VMEM((total + count_n, width), F32),
            jax.ShapeDtypeStruct((count_p, width), F32),
        ),
        in_specs=[smem(), smem()] + [hbm()] * 4,
        out_specs=(vmem(), hbm()),
        scratch_shapes=[
            pltpu.VMEM((remote_rows, count_n, width), BF16),
            pltpu.VMEM((classes, width, width), BF16),
            pltpu.VMEM((count_p, count_n, width), BF16),
            pltpu.VMEM((count_p, width), F32),
            pltpu.VMEM((count_p, width), F32),
            pltpu.VMEM((TILE * count_n, width), BF16),
            pltpu.VMEM((TILE * count_n, width), F32),
            pltpu.SemaphoreType.DMA((3,)),
            pltpu.SemaphoreType.DMA((classes,)),
            pltpu.SemaphoreType.DMA,
        ],
        compiler_params=params(56),
        cost_estimate=cost(2 * remote_rows * count_n * width * width, 14),
        name="remote_field",
    )(order, count, arrived, trans, cotangent, part)
    acc = stay(acc)

    mine = pl.pallas_call(
        functools.partial(combine, 1.0 / (count_n * dirs)),
        out_shape=jax.ShapeDtypeStruct((dirs, count_p // 2, 2 * width // dirs), F32),
        in_specs=[hbm()] * 3 + [vmem()],
        out_specs=vmem(),
        scratch_shapes=[
            pltpu.VMEM((remote_rows, LANES), F32),
            pltpu.VMEM((count_p, width), F32),
            pltpu.VMEM((count_p, width), F32),
            pltpu.SemaphoreType.DMA((3,)),
        ],
        compiler_params=params(24),
        cost_estimate=cost(row_ops, 1),
        name="combine",
    )(far_off(owner), far_off(mie), far_off(part), term)
    mine, field = lax.optimization_barrier((mine, field))
    amplitude = pl.pallas_call(
        amplitudes,
        out_shape=jax.ShapeDtypeStruct((count_p, count_n, width), BF16),
        in_specs=[vmem(), hbm(), hbm()],
        out_specs=hbm(),
        scratch_shapes=[
            pltpu.VMEM((total, width), F32),
            pltpu.VMEM((count_p, width), F32),
            pltpu.VMEM((count_p, count_n, width), BF16),
            pltpu.SemaphoreType.DMA((PARTS + 1,)),
            pltpu.SemaphoreType.DMA((PARTS,)),
        ],
        compiler_params=params(56),
        cost_estimate=cost(row_ops, 5),
        name="amplitudes",
    )(acc, field, mie)
    shares = lax.all_to_all(mine, "dir", split_axis=0, concat_axis=0, tiled=True)
    gradient = pl.pallas_call(
        add_shares,
        out_shape=jax.ShapeDtypeStruct((count_p, width // dirs), F32),
        in_specs=[vmem()],
        out_specs=vmem(),
        compiler_params=params(8),
        cost_estimate=cost(row_ops, 1),
        name="add_shares",
    )(shares)
    return amplitude, gradient


def solution(mesh):
    placed = (
        P("dom", "dir", None),
        P("dom", "dir", None),
        P("dom", None),
        P(),
        P("dom", None, None),
        P("dom", None),
    )
    return jax.shard_map(
        body,
        mesh=mesh,
        in_specs=placed,
        out_specs=(P("dom", "dir", None), P("dom", "dir")),
        check_vma=False,
    )
```

```python
import functools

import jax
import jax.numpy as jnp
from jax import lax
from jax.experimental import pallas as pl
from jax.experimental.pallas import tpu as pltpu
from jax.sharding import PartitionSpec as P

TILE = 32
WINDOW = 3
LANES = 128
NEAR = 128
SIZES = (16, 24, 32)
PARTS = 8
F32 = jnp.float32
BF16 = jnp.bfloat16
MIB = 1 << 20


def vmem():
    return pl.BlockSpec(memory_space=pltpu.VMEM)


def smem():
    return pl.BlockSpec(memory_space=pltpu.SMEM)


def hbm():
    return pl.BlockSpec(memory_space=pl.ANY)


def pack_rows(
    rows_hbm, mie_hbm, inc_hbm, out_hbm, rows_ref, mie_ref, inc_ref, start_ref, out_ref, in_sem, out_sem
):
    peers, cap = out_ref.shape[:2]
    part_peers = peers // PARTS
    pieces = in_sem.shape[0] - 2
    step = inc_ref.shape[0] // pieces

    def get(piece):
        here = pl.ds(piece * step, step)
        return pltpu.make_async_copy(inc_hbm.at[here], inc_ref.at[here], in_sem.at[piece])

    get_mie = pltpu.make_async_copy(mie_hbm, mie_ref, in_sem.at[pieces])
    get_rows = pltpu.make_async_copy(rows_hbm, rows_ref, in_sem.at[pieces + 1])
    get_mie.start()
    for piece in range(pieces):
        get(piece).start()
    get_rows.start()
    get_mie.wait()
    for piece in range(pieces):
        get(piece).wait()

        def scale(i, carry, piece=piece):
            p = piece * step + i
            start_ref[p] = (mie_ref[pl.ds(p, 1), :] * inc_ref[p].astype(F32)).astype(BF16)
            return carry

        lax.fori_loop(0, step, scale, 0, unroll=8)
    get_rows.wait()

    def put(part):
        here = pl.ds(part * part_peers, part_peers)
        return pltpu.make_async_copy(out_ref.at[here], out_hbm.at[here], out_sem.at[part])

    for part in range(PARTS):
        for i in range(part_peers):
            peer = part * part_peers + i
            for c in range(cap):
                out_ref[peer, c] = start_ref[rows_ref[c, peer]]
        put(part).start()
    for part in range(PARTS):
        put(part).wait()


def local_part(
    slot_ref,
    rows_ref,
    inc_hbm,
    cot_hbm,
    mie_hbm,
    trans_hbm,
    field_ref,
    near_ref,
    far_hbm,
    grad_ref,
    owner_ref,
    order_ref,
    count_ref,
    inc_ref,
    cot_ref,
    mie_ref,
    trans_ref,
    start_ref,
    adj_ref,
    lhs_ref,
    prod_ref,
    adjoint_ref,
    back_ref,
    in_sem,
    trans_sem,
    far_sem,
):
    count_p, count_n, width = inc_ref.shape
    classes = slot_ref.shape[0]
    stride = count_p + TILE
    dummy = back_ref.shape[0] - 1
    gets = [
        pltpu.make_async_copy(mie_hbm, mie_ref, in_sem.at[0]),
        pltpu.make_async_copy(inc_hbm, inc_ref, in_sem.at[1]),
        pltpu.make_async_copy(cot_hbm, cot_ref, in_sem.at[2]),
    ]

    def get_trans(k):
        return pltpu.make_async_copy(trans_hbm.at[k], trans_ref.at[k], trans_sem.at[k])

    for get in gets:
        get.start()
    for k in range(classes):
        get_trans(k).start()
    for get in gets:
        get.wait()

    def prepare(p, carry):
        scale = mie_ref[pl.ds(p, 1), :]
        inc = inc_ref[p].astype(F32)
        start_ref[p] = (scale * inc).astype(BF16)
        at = pl.multiple_of(p * count_n, count_n)
        adj_ref[pl.ds(at, count_n), :] = (scale * cot_ref[p].astype(F32)).astype(BF16)
        field_ref[pl.ds(at, count_n), :] = inc
        adjoint_ref[p] = jnp.zeros((count_n, width), F32)
        return carry

    lax.fori_loop(0, count_p, prepare, 0, unroll=4)
    start_ref[count_p] = jnp.zeros((count_n, width), BF16)
    adjoint_ref[count_p] = jnp.zeros((count_n, width), F32)

    def one_class(k, carry):
        base = k * stride

        def pick(p, tally):
            slot = slot_ref[k, p]
            is_local = (slot >= 0) & (slot < count_p)
            source = jnp.where(is_local, slot, count_p)
            at = pl.multiple_of(p * count_n, count_n)
            lhs_ref[pl.ds(at, count_n), :] = start_ref[source]
            remote = slot - count_p
            order_ref[base + tally] = remote * 128 + p
            return tally + (remote >= 0).astype(jnp.int32)

        tally = lax.fori_loop(0, count_p, pick, jnp.int32(0), unroll=4)
        count_ref[k] = tally
        for extra in range(TILE):
            order_ref[base + tally + extra] = count_p
        get_trans(k).wait()
        field_ref[...] += jnp.dot(lhs_ref[...], trans_ref[k], preferred_element_type=F32)
        prod_ref[...] = lax.dot_general(
            adj_ref[...],
            trans_ref[k],
            (((1,), (1,)), ((), ())),
            preferred_element_type=F32,
        )

        def spread(p, c):
            slot = slot_ref[k, p]
            is_local = (slot >= 0) & (slot < count_p)
            at = pl.multiple_of(p * count_n, count_n)
            prod = prod_ref[pl.ds(at, count_n), :]
            back_ref[jnp.where(slot >= count_p, slot - count_p, dummy)] = prod.astype(BF16)
            adjoint_ref[jnp.where(is_local, slot, count_p)] += prod
            return c

        lax.fori_loop(0, count_p, spread, 0, unroll=4)
        return carry

    lax.fori_loop(0, classes, one_class, 0)

    put_far = pltpu.make_async_copy(back_ref.at[pl.ds(NEAR, dummy - NEAR)], far_hbm, far_sem)
    put_far.start()

    def keep(i, carry):
        near_ref[i] = back_ref[i]
        return carry

    lax.fori_loop(0, NEAR, keep, 0, unroll=4)

    def own(q, carry):
        lane = lax.broadcasted_iota(jnp.int32, (1, LANES), 1)
        for c in range(rows_ref.shape[0]):
            owner_ref[pl.ds(q * rows_ref.shape[0] + c, 1), :] = (lane == rows_ref[c, q]).astype(F32)
        return carry

    lax.fori_loop(0, rows_ref.shape[1], own, 0)

    def finish(p, carry):
        at = pl.multiple_of(p * count_n, count_n)
        both = inc_ref[p].astype(F32) * adjoint_ref[p]
        both += cot_ref[p].astype(F32) * field_ref[pl.ds(at, count_n), :]
        grad_ref[pl.ds(p, 1), :] = jnp.sum(both, axis=0, keepdims=True)
        return carry

    lax.fori_loop(0, count_p, finish, 0, unroll=4)
    put_far.wait()


def remote_terms(arrived_hbm, far_hbm, back_ref, term_ref, near_ref, last_ref, far_ref, sem):
    peers, cap = term_ref.shape[:2]
    rows_in = peers * cap
    step = rows_in // PARTS
    parts_near = NEAR // step

    def get(part):
        start = part * step
        here = pl.ds(start, step)
        if part < parts_near:
            return [pltpu.make_async_copy(arrived_hbm.at[here], near_ref.at[here], sem.at[0, part])]
        there = pl.ds(start - NEAR, step)
        return [
            pltpu.make_async_copy(arrived_hbm.at[here], last_ref.at[there], sem.at[0, part]),
            pltpu.make_async_copy(far_hbm.at[there], far_ref.at[there], sem.at[1, part]),
        ]

    for part in range(PARTS):
        for copy in get(part):
            copy.start()
    for part in range(PARTS):
        for copy in get(part):
            copy.wait()
        is_near = part < parts_near
        got_ref, kept_ref = (near_ref, back_ref) if is_near else (last_ref, far_ref)
        base = part * step - (0 if is_near else NEAR)

        def one(i, carry, part=part, got_ref=got_ref, kept_ref=kept_ref, base=base):
            here = pl.ds(base + i * cap, cap)
            both = got_ref[here].astype(F32) * kept_ref[here].astype(F32)
            term_ref[part * (step // cap) + i] = jnp.sum(both, axis=1).astype(BF16)
            return carry

        lax.fori_loop(0, step // cap, one, 0)


def remote_field(
    scale,
    order_ref,
    count_ref,
    arrived_hbm,
    trans_hbm,
    cot_hbm,
    part_hbm,
    mie_hbm,
    owner_hbm,
    acc_ref,
    grad_ref,
    weight_ref,
    owner_ref,
    arrived_ref,
    trans_ref,
    cot_ref,
    part_ref,
    mie_ref,
    slots_ref,
    lhs_ref,
    moved_ref,
    in_sem,
    trans_sem,
):
    classes = trans_ref.shape[0]
    count_p, count_n, width = cot_ref.shape
    stride = count_p + TILE
    get_arrived = pltpu.make_async_copy(arrived_hbm, arrived_ref, in_sem.at[0])
    late = [
        pltpu.make_async_copy(cot_hbm, cot_ref, in_sem.at[1]),
        pltpu.make_async_copy(part_hbm, part_ref, in_sem.at[2]),
        pltpu.make_async_copy(mie_hbm, mie_ref, in_sem.at[3]),
        pltpu.make_async_copy(owner_hbm, slots_ref, in_sem.at[4]),
    ]

    def get_trans(k):
        return pltpu.make_async_copy(trans_hbm.at[k], trans_ref.at[k], trans_sem.at[k])

    get_arrived.start()
    for k in range(WINDOW):
        get_trans(k).start()

    def clear(p, carry):
        at = pl.multiple_of(p * count_n, count_n)
        acc_ref[pl.ds(at, count_n), :] = jnp.zeros((count_n, width), F32)
        return carry

    lax.fori_loop(0, count_p + 1, clear, 0, unroll=5)
    get_arrived.wait()

    def tile(k, first, size):
        base = k * stride + first
        for i in range(size):
            source = lax.shift_right_logical(order_ref[base + i], 7)
            lhs_ref[pl.ds(i * count_n, count_n), :] = arrived_ref[source]
        rows = pl.ds(0, size * count_n)
        moved_ref[rows, :] = jnp.dot(lhs_ref[rows, :], trans_ref[k], preferred_element_type=F32)
        for i in range(size):
            p = order_ref[base + i] & 127
            at = pl.multiple_of(p * count_n, count_n)
            acc_ref[pl.ds(at, count_n), :] += moved_ref[pl.ds(i * count_n, count_n), :]

    def fetch(k):
        get_trans(k).wait()

        @pl.when(k + WINDOW < classes)
        def _():
            get_trans(k + WINDOW).start()

        @pl.when(k + WINDOW == classes)
        def _():
            for get in late:
                get.start()

    def one_class(k, carry):
        fetch(k)
        count = count_ref[k]
        for low, size in zip((-1,) + SIZES, SIZES):
            here = count > low
            if size < TILE:
                here = here & (count <= size)

            @pl.when(here)
            def _(size=size):
                tile(k, 0, size)

        def more(t, c):
            tile(k, t * TILE, TILE)
            return c

        lax.fori_loop(1, lax.div(count + (TILE - 1), TILE), more, 0)
        return carry

    lax.fori_loop(0, classes, one_class, 0)
    for get in late:
        get.wait()

    weight_ref[...] = scale / mie_ref[...]
    owner_ref[...] = jnp.transpose(slots_ref[...]).astype(BF16)

    def finish(p, carry):
        at = pl.multiple_of(p * count_n, count_n)
        both = cot_ref[p].astype(F32) * acc_ref[pl.ds(at, count_n), :]
        summed = part_ref[pl.ds(p, 1), :] + jnp.sum(both, axis=0, keepdims=True)
        grad_ref[pl.ds(p, 1), :] = summed * scale
        return carry

    lax.fori_loop(0, count_p, finish, 0, unroll=4)


def amplitudes(acc_ref, field_hbm, mie_hbm, amp_hbm, field_ref, mie_ref, amp_ref, in_sem, out_sem):
    count_p, count_n, width = amp_ref.shape
    step = count_p // PARTS

    def get(part):
        here = pl.ds(part * step * count_n, step * count_n)
        return pltpu.make_async_copy(field_hbm.at[here], field_ref.at[here], in_sem.at[part])

    def put(part):
        here = pl.ds(part * step, step)
        return pltpu.make_async_copy(amp_ref.at[here], amp_hbm.at[here], out_sem.at[part])

    get_mie = pltpu.make_async_copy(mie_hbm, mie_ref, in_sem.at[PARTS])
    get_mie.start()
    for part in range(PARTS):
        get(part).start()
    get_mie.wait()
    for part in range(PARTS):
        get(part).wait()

        def one(i, carry, part=part):
            p = part * step + i
            here = pl.ds(pl.multiple_of(p * count_n, count_n), count_n)
            field = field_ref[here, :] + acc_ref[here, :]
            amp_ref[p] = (mie_ref[pl.ds(p, 1), :] * field).astype(BF16)
            return carry

        lax.fori_loop(0, step, one, 0, unroll=4)
        put(part).start()
    for part in range(PARTS):
        put(part).wait()


def combine(owner_ref, weight_ref, part_ref, term_ref, out_ref):
    count_p, width = weight_ref.shape
    mine = jnp.dot(
        owner_ref[...],
        term_ref[...].reshape(owner_ref.shape[1], width),
        preferred_element_type=F32,
    )
    whole = part_ref[...] + mine[:count_p] * weight_ref[...]
    dirs, half, pair = out_ref.shape
    share = pair // 2
    for r in range(dirs):
        block = whole[:, r * share : (r + 1) * share]
        out_ref[r] = jnp.concatenate([block[:half], block[half:]], axis=1)


def add_shares(in_ref, out_ref):
    summed = jnp.sum(in_ref[...], axis=0)
    share = summed.shape[1] // 2
    out_ref[...] = jnp.concatenate([summed[:, :share], summed[:, share:]], axis=0)


def params(mib=60):
    return pltpu.CompilerParams(vmem_limit_bytes=mib * MIB)


def cost(flops, mib):
    return pl.CostEstimate(flops=int(flops), bytes_accessed=mib * MIB, transcendentals=0)


def stay(x):
    return pltpu.with_memory_space_constraint(x, pltpu.VMEM)


def body(incident, cotangent, mie, trans, send_rows, partner_slot):
    count_p, count_n, width = incident.shape
    classes = trans.shape[0]
    peers = lax.axis_size("dom")
    dirs = lax.axis_size("dir")
    cap = send_rows.shape[2]
    remote_rows = peers * cap
    total = count_p * count_n
    row_ops = count_p * count_n * width

    rows = jnp.transpose(send_rows[0])
    slots = jnp.transpose(partner_slot)

    def send(x):
        return lax.all_to_all(x, "dom", split_axis=0, concat_axis=0, tiled=True)

    packed = pl.pallas_call(
        pack_rows,
        out_shape=jax.ShapeDtypeStruct((peers, cap, count_n, width), BF16),
        in_specs=[hbm()] * 3,
        out_specs=hbm(),
        scratch_shapes=[
            pltpu.SMEM((cap, peers), jnp.int32),
            pltpu.VMEM((count_p, width), F32),
            pltpu.VMEM((count_p, count_n, width), BF16),
            pltpu.VMEM((count_p, count_n, width), BF16),
            pltpu.VMEM((peers, cap, count_n, width), BF16),
            pltpu.SemaphoreType.DMA((6,)),
            pltpu.SemaphoreType.DMA((PARTS,)),
        ],
        compiler_params=params(),
        cost_estimate=cost(row_ops, 4),
        name="pack_rows",
    )(rows, mie, incident)
    arrived = send(packed).reshape(remote_rows, count_n, width)

    far_rows = remote_rows - NEAR
    field, near, far, part, owner, order, count = pl.pallas_call(
        local_part,
        out_shape=(
            jax.ShapeDtypeStruct((total, width), F32),
            pltpu.VMEM((NEAR, count_n, width), BF16),
            jax.ShapeDtypeStruct((far_rows, count_n, width), BF16),
            jax.ShapeDtypeStruct((count_p, width), F32),
            jax.ShapeDtypeStruct((remote_rows, LANES), F32),
            jax.ShapeDtypeStruct((classes * (count_p + TILE),), jnp.int32),
            jax.ShapeDtypeStruct((classes,), jnp.int32),
        ),
        in_specs=[smem(), smem()] + [hbm()] * 4,
        out_specs=(vmem(), vmem(), hbm(), vmem(), vmem(), smem(), smem()),
        scratch_shapes=[
            pltpu.VMEM((count_p, count_n, width), BF16),
            pltpu.VMEM((count_p, count_n, width), BF16),
            pltpu.VMEM((count_p, width), F32),
            pltpu.VMEM((classes, width, width), BF16),
            pltpu.VMEM((count_p + 1, count_n, width), BF16),
            pltpu.VMEM((total, width), BF16),
            pltpu.VMEM((total, width), BF16),
            pltpu.VMEM((total, width), F32),
            pltpu.VMEM((count_p + 1, count_n, width), F32),
            pltpu.VMEM((remote_rows + 1, count_n, width), BF16),
            pltpu.SemaphoreType.DMA((3,)),
            pltpu.SemaphoreType.DMA((classes,)),
            pltpu.SemaphoreType.DMA,
        ],
        compiler_params=params(),
        cost_estimate=cost(4 * classes * row_ops * width, 16),
        name="local_part",
    )(slots, rows, incident, cotangent, mie, trans)
    near = stay(near)

    term = pl.pallas_call(
        remote_terms,
        out_shape=jax.ShapeDtypeStruct((peers, cap, width), BF16),
        in_specs=[hbm(), hbm(), vmem()],
        out_specs=vmem(),
        scratch_shapes=[
            pltpu.VMEM((NEAR, count_n, width), BF16),
            pltpu.VMEM((far_rows, count_n, width), BF16),
            pltpu.VMEM((far_rows, count_n, width), BF16),
            pltpu.SemaphoreType.DMA((2, PARTS)),
        ],
        compiler_params=params(58),
        cost_estimate=cost(4 * row_ops, 8),
        name="remote_terms",
    )(arrived, far, near)
    term = send(term)

    acc, part, weight, owner_near = pl.pallas_call(
        functools.partial(remote_field, 1.0 / (count_n * dirs)),
        out_shape=(
            pltpu.VMEM((total + count_n, width), F32),
            pltpu.VMEM((count_p, width), F32),
            pltpu.VMEM((count_p, width), F32),
            pltpu.VMEM((LANES, remote_rows), BF16),
        ),
        in_specs=[smem(), smem()] + [hbm()] * 6,
        out_specs=(vmem(),) * 4,
        scratch_shapes=[
            pltpu.VMEM((remote_rows, count_n, width), BF16),
            pltpu.VMEM((classes, width, width), BF16),
            pltpu.VMEM((count_p, count_n, width), BF16),
            pltpu.VMEM((count_p, width), F32),
            pltpu.VMEM((count_p, width), F32),
            pltpu.VMEM((remote_rows, LANES), F32),
            pltpu.VMEM((TILE * count_n, width), BF16),
            pltpu.VMEM((TILE * count_n, width), F32),
            pltpu.SemaphoreType.DMA((5,)),
            pltpu.SemaphoreType.DMA((classes,)),
        ],
        compiler_params=params(56),
        cost_estimate=cost(2 * remote_rows * count_n * width * width, 14),
        name="remote_field",
    )(order, count, arrived, trans, cotangent, part, mie, owner)
    acc, part, weight, owner_near = (stay(x) for x in (acc, part, weight, owner_near))

    mine = pl.pallas_call(
        combine,
        out_shape=jax.ShapeDtypeStruct((dirs, count_p // 2, 2 * width // dirs), F32),
        in_specs=[vmem()] * 4,
        out_specs=vmem(),
        compiler_params=params(24),
        cost_estimate=cost(row_ops, 1),
        name="combine",
    )(owner_near, weight, part, term)
    mine, field = lax.optimization_barrier((mine, field))
    amplitude = pl.pallas_call(
        amplitudes,
        out_shape=jax.ShapeDtypeStruct((count_p, count_n, width), BF16),
        in_specs=[vmem(), hbm(), hbm()],
        out_specs=hbm(),
        scratch_shapes=[
            pltpu.VMEM((total, width), F32),
            pltpu.VMEM((count_p, width), F32),
            pltpu.VMEM((count_p, count_n, width), BF16),
            pltpu.SemaphoreType.DMA((PARTS + 1,)),
            pltpu.SemaphoreType.DMA((PARTS,)),
        ],
        compiler_params=params(56),
        cost_estimate=cost(row_ops, 5),
        name="amplitudes",
    )(acc, field, mie)
    shares = lax.all_to_all(mine, "dir", split_axis=0, concat_axis=0, tiled=True)
    gradient = pl.pallas_call(
        add_shares,
        out_shape=jax.ShapeDtypeStruct((count_p, width // dirs), F32),
        in_specs=[vmem()],
        out_specs=vmem(),
        compiler_params=params(8),
        cost_estimate=cost(row_ops, 1),
        name="add_shares",
    )(shares)
    return amplitude, gradient


def solution(mesh):
    placed = (
        P("dom", "dir", None),
        P("dom", "dir", None),
        P("dom", None),
        P(),
        P("dom", None, None),
        P("dom", None),
    )
    return jax.shard_map(
        body,
        mesh=mesh,
        in_specs=placed,
        out_specs=(P("dom", "dir", None), P("dom", "dir")),
        check_vma=False,
    )
```
